512 devices in a mesh: row: 32 (over x_lo, z), col: 16 (over x_hi, y, core).
Axes of the slice: x: 4 (x_hi: 2, x_lo: 2; x = x_hi * 2 + x_lo), y: 4, z: 16, core: 2. Of those that a mesh axis runs over, the one named last changes fastest.
Arguments:
- a_blocks: bfloat16 [32, 16, 80, 128, 128], P('row', 'col'), may hold values from -6 to 6
- a_rows: int32 [32, 16, 80], P('row', 'col'), may hold values from 0 to 7, as said below
- a_cols: int32 [32, 16, 80], P('row', 'col'), may hold values from 0 to 15, as said below
- a_count: int32 [32, 16], P('row', 'col'), may hold values from 27 to 80, as said below
- b_blocks: bfloat16 [32, 16, 20, 128, 128], P('row', 'col'), may hold values from -0.125 to 0.125
- b_rows: int32 [32, 16, 20], P('row', 'col'), may hold values from 0 to 15, as said below
- b_cols: int32 [32, 16, 20], P('row', 'col'), may hold values from 0 to 1, as said below
- b_count: int32 [32, 16], P('row', 'col'), may hold values from 7 to 20, as said below
Outputs:
- c_slab: bfloat16 [32768, 4096], P('row', 'col')
The draws below stay inside these ranges and needn't reach their ends.
Inputs may be any that keep to these rules, and one draw needn't show every extreme that they name: `a_rows`: within one panel the live slots name distinct blocks; slots at or past the count hold blocks that are not used, with indices in range. `a_cols`: paired slot by slot with a_rows. `a_count`: some panel is full in every draw. `b_rows`: within one panel the live slots name distinct blocks; slots at or past the count hold blocks that are not used, with indices in range. `b_cols`: paired slot by slot with b_rows. `b_count`: some panel is full in every draw.
All inputs are finite; a program needn't handle non-finite values.
Results may differ from the reference program's by a relative error of at most 0.001.
Values may be sent and summed in bfloat16 or wider, within the bound.
A program may use at most 128 MiB of HBM per device.

```python
import jax
import jax.numpy as jnp
from jax import lax

BS = 128
RB = 8
KB = 16
CB = 2
STEPS = 4
PAD_A = 80
PAD_B = 20
GRID_ROWS = 32
GRID_COLS = 16


def cell_picks(key, block_rows, block_cols, slots):
    key_list = jax.random.split(key, GRID_ROWS * GRID_COLS)
    shuffled = jax.vmap(lambda one_key: jax.random.permutation(one_key, block_rows * block_cols))(key_list)
    return shuffled[:, :slots].reshape(GRID_ROWS, GRID_COLS, slots).astype(jnp.int32)


def live_counts(key, slots):
    counts = jax.random.randint(key, (GRID_ROWS * GRID_COLS,), (slots + 2) // 3, slots + 1, dtype=jnp.int32)
    chosen = jax.random.randint(jax.random.fold_in(key, 5), (), 0, GRID_ROWS * GRID_COLS, dtype=jnp.int32)
    counts = jnp.where(jnp.arange(GRID_ROWS * GRID_COLS, dtype=jnp.int32) == chosen, slots, counts)
    return counts.reshape(GRID_ROWS, GRID_COLS)


def draw_a_rows(key, part):
    return cell_picks(jax.random.fold_in(key, 11), RB, KB, PAD_A) // KB


def draw_a_cols(key, part):
    return cell_picks(jax.random.fold_in(key, 11), RB, KB, PAD_A) % KB


def draw_a_count(key, part):
    key = jax.random.fold_in(key, 3)
    return live_counts(key, PAD_A)


def draw_b_rows(key, part):
    return cell_picks(jax.random.fold_in(key, 13), KB, CB, PAD_B) // CB


def draw_b_cols(key, part):
    return cell_picks(jax.random.fold_in(key, 13), KB, CB, PAD_B) % CB


def draw_b_count(key, part):
    key = jax.random.fold_in(key, 7)
    return live_counts(key, PAD_B)


def level_of(key, extent, pieces, least, largest):
    level, own = 1.0, jax.random.fold_in(key, 6)
    for axis_at, shards_of in pieces:
        draws = jnp.exp(jax.random.uniform(jax.random.fold_in(own, axis_at), (shards_of,), jnp.float32, least / len(pieces), largest / len(pieces)))
        level = level * jnp.repeat(draws, extent[axis_at] // shards_of).reshape([-1 if axis == axis_at else 1 for axis in range(len(extent))])
    return level


def gaussian(rng, extent, scale, limit, pieces=(), kind=jnp.bfloat16):
    factor_of = level_of(rng, extent, pieces, -0.22, 0.18) if pieces else 1.0
    drawn = jax.random.normal(rng, extent, jnp.float32) * scale * factor_of
    return jnp.minimum(jnp.maximum(drawn, -limit), limit).astype(kind)


def setup_inputs(seed: int = 0) -> dict:
    arg_keys = jax.random.split(jax.random.key(seed), 9)
    return {
        "a_blocks": gaussian(arg_keys[0], (GRID_ROWS, GRID_COLS, PAD_A, BS, BS), 1.0, 6.0, ((0, 32), (1, 16))),
        "a_rows": draw_a_rows(jax.random.fold_in(arg_keys[8], 71), 0),
        "a_cols": draw_a_cols(jax.random.fold_in(arg_keys[8], 71), 0),
        "a_count": draw_a_count(jax.random.fold_in(arg_keys[8], 71), 0),
        "b_blocks": gaussian(arg_keys[4], (GRID_ROWS, GRID_COLS, PAD_B, BS, BS), (KB * BS) ** -0.5, 0.125, ((0, 32), (1, 16))),
        "b_rows": draw_b_rows(jax.random.fold_in(arg_keys[8], 71), 0),
        "b_cols": draw_b_cols(jax.random.fold_in(arg_keys[8], 71), 0),
        "b_count": draw_b_count(jax.random.fold_in(arg_keys[8], 71), 0),
    }


def densify(blocks, rows, cols, count, block_rows, block_cols):
    slots = jnp.arange(blocks.shape[0], dtype=jnp.int32)
    live = (slots < count).astype(jnp.float32)
    row_hot = (rows[:, None] == jnp.arange(block_rows, dtype=jnp.int32)[None, :]).astype(jnp.float32) * live[:, None]
    col_hot = (cols[:, None] == jnp.arange(block_cols, dtype=jnp.int32)[None, :]).astype(jnp.float32)
    dense = jnp.einsum("pr,pc,pxy->rxcy", row_hot, col_hot, blocks.astype(jnp.float32),
                       precision=lax.Precision.HIGHEST)
    return dense.reshape(block_rows * BS, block_cols * BS).astype(jnp.bfloat16)


def reference(a_blocks, a_rows, a_cols, a_count, b_blocks, b_rows, b_cols, b_count):
    def dense_a_row(grid_row):
        return jax.vmap(lambda blocks, rows, cols, count: densify(blocks, rows, cols, count, RB, KB))(
            a_blocks[grid_row], a_rows[grid_row], a_cols[grid_row], a_count[grid_row])

    def dense_b_row(grid_row):
        return jax.vmap(lambda blocks, rows, cols, count: densify(blocks, rows, cols, count, KB, CB))(
            b_blocks[grid_row], b_rows[grid_row], b_cols[grid_row], b_count[grid_row])

    every_row = jnp.arange(GRID_ROWS, dtype=jnp.int32)
    dense_a = lax.map(dense_a_row, every_row)
    dense_b = lax.map(dense_b_row, every_row)

    def one_row(grid_row):
        total = jnp.zeros((GRID_COLS, RB * BS, CB * BS), jnp.float32)
        for shift_step in range(STEPS):
            a_here = jnp.roll(dense_a[grid_row], -shift_step, axis=0)
            b_here = dense_b[(grid_row + shift_step) % GRID_ROWS]
            total = total + jnp.einsum("jrk,jkc->jrc", a_here.astype(jnp.float32), b_here.astype(jnp.float32),
                                       precision=lax.Precision.HIGHEST)
        return total.astype(jnp.bfloat16)

    tiles = lax.map(one_row, every_row)
    return tiles.transpose(0, 2, 1, 3).reshape(GRID_ROWS * RB * BS, GRID_COLS * CB * BS)
```

```python
import functools

import jax
import jax.numpy as jnp
from jax import lax
from jax.experimental import pallas as pl
from jax.experimental.pallas import tpu as pltpu
from jax.sharding import PartitionSpec as P

RB = 8
KB = 16
CB = 2
STEPS = 4
CHUNKS = 4
TILES = 4
WIDE = False

MESH = pl.DeviceIdType.MESH


def slot_codes(rows_ref, cols_ref, count_ref, block_cols):
    slots = lax.broadcasted_iota(jnp.int32, rows_ref.shape, 1)
    codes = rows_ref[...] * block_cols + cols_ref[...]
    return jnp.where(slots < count_ref[0, 0], codes, -1)


def slot_of_block(codes, blocks, empty):
    width = codes.shape[1]
    wanted = lax.broadcasted_iota(jnp.int32, (blocks, width), 0)
    slots = lax.broadcasted_iota(jnp.int32, (blocks, width), 1)
    hits = jnp.where(jnp.broadcast_to(codes, (blocks, width)) == wanted, slots, empty)
    return jnp.broadcast_to(jnp.min(hits, axis=1, keepdims=True), (blocks, 128))


def kernel(
    grid_rows,
    grid_cols,
    a_rows,
    a_cols,
    a_count,
    b_rows,
    b_cols,
    b_count,
    a_blocks,
    b_blocks,
    out_ref,
    a_held,
    a_dense,
    b_own,
    b_one,
    b_two,
    b_three,
    b_dense,
    codes,
    found_a,
    found_b,
    where_a,
    where_b,
    total,
    t_out,
    t_in,
    scale_out,
    scale_in,
    local_sem,
    b_send,
    b_recv,
    t_send,
    t_recv,
):
    pad_a, bs = a_blocks.shape[0], a_blocks.shape[1]
    pad_b = b_blocks.shape[0]
    part = pad_b // CHUNKS
    tile = RB * bs // TILES
    b_held = (b_own, b_one, b_two, b_three)
    i, k = lax.axis_index("row"), lax.axis_index("col")

    def at_col(distance):
        return (i, lax.rem(k + distance + grid_cols, grid_cols))

    onward = (lax.rem(i + grid_rows - 1, grid_rows), lax.rem(k + 1, grid_cols))
    origin = (lax.rem(i + 1, grid_rows), lax.rem(k + grid_cols - 1, grid_cols))

    a_held[pad_a] = jnp.zeros((bs, bs), jnp.bfloat16)
    for held in b_held:
        held[pad_b] = jnp.zeros((bs, bs), jnp.bfloat16)

    barrier = pltpu.get_barrier_semaphore()
    pl.semaphore_signal(barrier, inc=1, device_id=origin, device_id_type=MESH)
    for s in range(1, STEPS):
        pl.semaphore_signal(barrier, inc=1, device_id=at_col(s), device_id_type=MESH)

    b_load = pltpu.make_async_copy(b_blocks, b_own.at[pl.ds(0, pad_b)], local_sem.at[0])
    b_load.start()
    a_load = pltpu.make_async_copy(a_blocks, a_held.at[pl.ds(0, pad_a)], local_sem.at[1])
    a_load.start()

    codes[0] = jnp.full((8, 128), -1, jnp.int32)
    codes[0, 0:1, 0:pad_b] = slot_codes(b_rows, b_cols, b_count, CB)

    def code_hop(s):
        return pltpu.make_async_remote_copy(
            src_ref=codes.at[s],
            dst_ref=codes.at[s + 1],
            send_sem=b_send.at[s, CHUNKS],
            recv_sem=b_recv.at[s, CHUNKS],
            device_id=onward,
            device_id_type=MESH,
        )

    def chunk_hop(s, c):
        span = pl.ds(c * part, part)
        return pltpu.make_async_remote_copy(
            src_ref=b_blocks.at[span] if s == 0 else b_held[s].at[span],
            dst_ref=b_held[s + 1].at[span],
            send_sem=b_send.at[s, c],
            recv_sem=b_recv.at[s, c],
            device_id=onward,
            device_id_type=MESH,
        )

    def tile_home(s, t):
        span = pl.ds(pl.multiple_of(t * tile, tile), tile)
        return pltpu.make_async_remote_copy(
            src_ref=t_out.at[s - 1, span],
            dst_ref=t_in.at[s - 1, span],
            send_sem=t_send.at[s - 1, t, 0],
            recv_sem=t_recv.at[s - 1, t, 0],
            device_id=at_col(-s),
            device_id_type=MESH,
        )

    def scale_home(s, t):
        return pltpu.make_async_remote_copy(
            src_ref=scale_out.at[s - 1, t],
            dst_ref=scale_in.at[s - 1, t],
            send_sem=t_send.at[s - 1, t, 1],
            recv_sem=t_recv.at[s - 1, t, 1],
            device_id=at_col(-s),
            device_id_type=MESH,
        )

    pl.semaphore_wait(barrier, STEPS)
    code_hop(0).start()
    for c in range(CHUNKS):
        chunk_hop(0, c).start()

    found_a[...] = slot_of_block(slot_codes(a_rows, a_cols, a_count, KB), RB * KB, pad_a)
    a_table = pltpu.make_async_copy(found_a, where_a, local_sem.at[2])
    a_table.start()
    a_table.wait()
    a_load.wait()

    def place_a(p, carry):
        r, c = p // KB, p % KB
        a_dense[
            pl.ds(pl.multiple_of(r * bs, bs), bs), pl.ds(pl.multiple_of(c * bs, bs), bs)
        ] = a_held[where_a[p, 0]]
        return carry

    lax.fori_loop(0, RB * KB, place_a, 0)

    def dense_b(s):
        found_b[...] = slot_of_block(codes[s, 0:1, :], KB * CB, pad_b)
        b_table = pltpu.make_async_copy(found_b, where_b, local_sem.at[3])
        b_table.start()
        b_table.wait()

        def place_b(p, carry):
            r, c = p // CB, p % CB
            b_dense[
                pl.ds(pl.multiple_of(r * bs, bs), bs), pl.ds(pl.multiple_of(c * bs, bs), bs)
            ] = b_held[s][where_b[p, 0]]
            return carry

        lax.fori_loop(0, KB * CB, place_b, 0)

    def product(t):
        rows = pl.ds(pl.multiple_of(t * tile, tile), tile)
        return jnp.dot(a_dense[rows, :], b_dense[...], preferred_element_type=jnp.float32)

    def own_tile(t, carry):
        rows = pl.ds(pl.multiple_of(t * tile, tile), tile)
        total[rows, :] = product(t)
        return carry

    b_load.wait()
    dense_b(0)
    lax.fori_loop(0, TILES, own_tile, 0)

    def term_from(s, t):
        rows = pl.ds(pl.multiple_of(t * tile, tile), tile)
        tile_home(s, t).wait_recv()
        if WIDE:
            return t_in[s - 1, rows, :]
        scale_home(s, t).wait_recv()
        return t_in[s - 1, rows, :].astype(jnp.float32) * scale_in[s - 1, t]

    def add_tile(s, t, carry):
        rows = pl.ds(pl.multiple_of(t * tile, tile), tile)
        total[rows, :] = total[rows, :] + term_from(s, t)
        return carry

    def last_tile(t, carry):
        rows = pl.ds(pl.multiple_of(t * tile, tile), tile)
        out_ref[rows, :] = (total[rows, :] + term_from(STEPS - 1, t)).astype(jnp.bfloat16)
        return carry

    def sent_tile(s, t, carry):
        rows = pl.ds(pl.multiple_of(t * tile, tile), tile)
        term = product(t)
        if WIDE:
            t_out[s - 1, rows, :] = term
        else:
            largest = jnp.maximum(jnp.max(jnp.abs(term), axis=0, keepdims=True), 1e-30)
            scale_out[s - 1, t] = largest * (1.0 / 32767.0)
            scale_home(s, t).start()
            coded = jnp.round(term * (32767.0 / largest))
            t_out[s - 1, rows, :] = coded.astype(jnp.int32).astype(jnp.int16)
        tile_home(s, t).start()
        return carry

    for s in range(1, STEPS):
        code_hop(s - 1).wait_recv()
        if s < STEPS - 1:
            code_hop(s).start()
        for c in range(CHUNKS):
            chunk_hop(s - 1, c).wait_recv()
            if s < STEPS - 1:
                chunk_hop(s, c).start()
        dense_b(s)
        lax.fori_loop(0, TILES, functools.partial(sent_tile, s), 0)
        if s > 1:
            lax.fori_loop(0, TILES, functools.partial(add_tile, s - 1), 0)
    lax.fori_loop(0, TILES, last_tile, 0)

    for s in range(STEPS - 1):
        code_hop(s).wait_send()
        for c in range(CHUNKS):
            chunk_hop(s, c).wait_send()
        for t in range(TILES):
            tile_home(s + 1, t).wait_send()
            if not WIDE:
                scale_home(s + 1, t).wait_send()


def per_device(a_blocks, a_rows, a_cols, a_count, b_blocks, b_rows, b_cols, b_count):
    grid_rows, grid_cols = lax.axis_size("row"), lax.axis_size("col")
    pad_a, bs = a_blocks.shape[2], a_blocks.shape[3]
    pad_b = b_blocks.shape[2]
    sent = jnp.float32 if WIDE else jnp.int16
    vmem = pl.BlockSpec(memory_space=pltpu.VMEM)
    smem = pl.BlockSpec(memory_space=pltpu.SMEM)
    whole = pl.BlockSpec(memory_space=pl.ANY)
    rows, depth, columns = RB * bs, KB * bs, CB * bs
    return pl.pallas_call(
        functools.partial(kernel, grid_rows, grid_cols),
        out_shape=jax.ShapeDtypeStruct((rows, columns), jnp.bfloat16),
        in_specs=[vmem, vmem, smem, vmem, vmem, smem, whole, whole],
        out_specs=vmem,
        scratch_shapes=[
            pltpu.VMEM((pad_a + 1, bs, bs), jnp.bfloat16),
            pltpu.VMEM((rows, depth), jnp.bfloat16),
            *[pltpu.VMEM((pad_b + 1, bs, bs), jnp.bfloat16)] * STEPS,
            pltpu.VMEM((depth, columns), jnp.bfloat16),
            pltpu.VMEM((STEPS, 8, 128), jnp.int32),
            pltpu.VMEM((RB * KB, 128), jnp.int32),
            pltpu.VMEM((KB * CB, 128), jnp.int32),
            pltpu.SMEM((RB * KB, 128), jnp.int32),
            pltpu.SMEM((KB * CB, 128), jnp.int32),
            pltpu.VMEM((rows, columns), jnp.float32),
            pltpu.VMEM((STEPS - 1, rows, columns), sent),
            pltpu.VMEM((STEPS - 1, rows, columns), sent),
            pltpu.VMEM((STEPS - 1, TILES, 1, columns), jnp.float32),
            pltpu.VMEM((STEPS - 1, TILES, 1, columns), jnp.float32),
            pltpu.SemaphoreType.DMA((4,)),
            pltpu.SemaphoreType.DMA((STEPS - 1, CHUNKS + 1)),
            pltpu.SemaphoreType.DMA((STEPS - 1, CHUNKS + 1)),
            pltpu.SemaphoreType.DMA((STEPS - 1, TILES, 2)),
            pltpu.SemaphoreType.DMA((STEPS - 1, TILES, 2)),
        ],
        compiler_params=pltpu.CompilerParams(
            collective_id=0, has_side_effects=True, vmem_limit_bytes=48 * 1024 * 1024
        ),
    )(
        a_rows.reshape(1, pad_a),
        a_cols.reshape(1, pad_a),
        a_count,
        b_rows.reshape(1, pad_b),
        b_cols.reshape(1, pad_b),
        b_count,
        a_blocks.reshape(pad_a, bs, bs),
        b_blocks.reshape(pad_b, bs, bs),
    )


def solution(mesh):
    placed = (
        P("row", "col", None, None, None),
        P("row", "col", None),
        P("row", "col", None),
        P("row", "col"),
        P("row", "col", None, None, None),
        P("row", "col", None),
        P("row", "col", None),
        P("row", "col"),
    )
    return jax.shard_map(
        per_device, mesh=mesh, in_specs=placed, out_specs=P("row", "col"), check_vma=False
    )
```

```python
import functools

import jax
import jax.numpy as jnp
from jax import lax
from jax.experimental import pallas as pl
from jax.experimental.pallas import tpu as pltpu
from jax.sharding import PartitionSpec as P

RB = 8
KB = 16
CB = 2
STEPS = 4
HALVES = 2
TILES = 2

MESH = pl.DeviceIdType.MESH


def slot_codes(rows_ref, cols_ref, count_ref, block_cols):
    slots = lax.broadcasted_iota(jnp.int32, rows_ref.shape, 1)
    codes = rows_ref[...] * block_cols + cols_ref[...]
    return jnp.where(slots < count_ref[0, 0], codes, -1)


def slot_of_block(codes, blocks, empty):
    width = codes.shape[1]
    wanted = lax.broadcasted_iota(jnp.int32, (blocks, width), 0)
    slots = lax.broadcasted_iota(jnp.int32, (blocks, width), 1)
    hits = jnp.where(jnp.broadcast_to(codes, (blocks, width)) == wanted, slots, empty)
    return jnp.broadcast_to(jnp.min(hits, axis=1, keepdims=True), (blocks, 128))


def kernel(
    grid_rows,
    grid_cols,
    a_rows_hbm,
    a_cols_hbm,
    a_count,
    b_rows_hbm,
    b_cols_hbm,
    b_count,
    a_blocks,
    b_blocks,
    out_ref,
    a_rows,
    a_cols,
    b_rows,
    b_cols,
    a_held,
    a_dense,
    b_raw,
    own_0,
    own_1,
    one_0,
    one_1,
    two_0,
    two_1,
    three_0,
    three_1,
    b_dense,
    codes,
    found_a,
    found_b,
    where_a,
    where_b,
    total,
    t_out,
    t_in,
    scale_out,
    scale_in,
    passed,
    local_sem,
    table_sem,
    b_send,
    b_recv,
    pass_send,
    pass_recv,
    t_send,
    t_recv,
):
    pad_a, bs = a_blocks.shape[0], a_blocks.shape[1]
    pad_b = b_blocks.shape[0]
    strip = bs // HALVES
    tile = RB * bs // TILES
    b_held = ((own_0, own_1), (one_0, one_1), (two_0, two_1), (three_0, three_1))
    i, k = lax.axis_index("row"), lax.axis_index("col")

    def at_col(distance):
        return (i, lax.rem(k + distance + grid_cols, grid_cols))

    onward = (lax.rem(i + grid_rows - 1, grid_rows), lax.rem(k + 1, grid_cols))
    origin = (lax.rem(i + 1, grid_rows), lax.rem(k + grid_cols - 1, grid_cols))

    run = grid_rows // 2
    at_first, at_last = lax.rem(i, run) == 0, lax.rem(i, run) == run - 1
    beside = (lax.rem(i + run, grid_rows), k)
    past_beside = (lax.rem(i + run + grid_rows - 1, grid_rows), lax.rem(k + 1, grid_cols))
    passes_here = (lax.rem(i + 1 + run, grid_rows), lax.rem(k + grid_cols - 1, grid_cols))

    nothing = jnp.zeros((strip, bs), jnp.bfloat16)
    for held in b_held:
        for h in range(HALVES):
            held[h][pad_b] = nothing
    a_held[pad_a] = jnp.zeros((bs, bs), jnp.bfloat16)

    barrier = pltpu.get_barrier_semaphore()
    pl.semaphore_signal(barrier, inc=1, device_id=origin, device_id_type=MESH)
    for s in range(1, STEPS):
        pl.semaphore_signal(barrier, inc=1, device_id=at_col(s), device_id_type=MESH)

    @pl.when(at_last)
    def _():
        pl.semaphore_signal(barrier, inc=1, device_id=passes_here, device_id_type=MESH)

    @pl.when(at_first)
    def _():
        pl.semaphore_signal(barrier, inc=1, device_id=beside, device_id_type=MESH)

    loads = [
        pltpu.make_async_copy(source, target, local_sem.at[n])
        for n, (source, target) in enumerate(
            (
                (b_blocks, b_raw),
                (b_rows_hbm, b_rows),
                (b_cols_hbm, b_cols),
                (a_rows_hbm, a_rows),
                (a_cols_hbm, a_cols),
                (a_blocks, a_held.at[pl.ds(0, pad_a)]),
            )
        )
    ]
    for load in loads:
        load.start()

    def code_hop(s):
        return pltpu.make_async_remote_copy(
            src_ref=codes.at[s],
            dst_ref=codes.at[s + 1],
            send_sem=b_send.at[s, HALVES],
            recv_sem=b_recv.at[s, HALVES],
            device_id=onward,
            device_id_type=MESH,
        )

    def half_hop(s, h):
        return pltpu.make_async_remote_copy(
            src_ref=b_held[s][h].at[pl.ds(0, pad_b)],
            dst_ref=b_held[s + 1][h].at[pl.ds(0, pad_b)],
            send_sem=b_send.at[s, h],
            recv_sem=b_recv.at[s, h],
            device_id=onward,
            device_id_type=MESH,
        )

    def hop_beside(s):
        return pltpu.make_async_remote_copy(
            src_ref=b_held[s][HALVES - 1].at[pl.ds(0, pad_b)],
            dst_ref=passed.at[s],
            send_sem=b_send.at[s, HALVES - 1],
            recv_sem=pass_recv.at[s],
            device_id=beside,
            device_id_type=MESH,
        )

    def pass_on(s):
        return pltpu.make_async_remote_copy(
            src_ref=passed.at[s],
            dst_ref=b_held[s + 1][HALVES - 1].at[pl.ds(0, pad_b)],
            send_sem=pass_send.at[s],
            recv_sem=b_recv.at[s, HALVES - 1],
            device_id=past_beside,
            device_id_type=MESH,
        )

    def start_half(s, h):
        if h < HALVES - 1:
            half_hop(s, h).start()
            return

        @pl.when(at_first)
        def _():
            hop_beside(s).start()

        @pl.when(jnp.logical_not(at_first))
        def _():
            half_hop(s, h).start()

    def start_pass(s):
        @pl.when(at_first)
        def _():
            hop_beside(s).wait_recv()
            pass_on(s).start()

    def tile_rows(t):
        return pl.ds(pl.multiple_of(t * tile, tile), tile)

    def tile_home(s, h, t):
        return pltpu.make_async_remote_copy(
            src_ref=t_out.at[s - 1, h, tile_rows(t)],
            dst_ref=t_in.at[s - 1, h, tile_rows(t)],
            send_sem=t_send.at[s - 1, h, t, 0],
            recv_sem=t_recv.at[s - 1, h, t, 0],
            device_id=at_col(-s),
            device_id_type=MESH,
        )

    def scale_home(s, h, t):
        return pltpu.make_async_remote_copy(
            src_ref=scale_out.at[s - 1, h, t],
            dst_ref=scale_in.at[s - 1, h, t],
            send_sem=t_send.at[s - 1, h, t, 1],
            recv_sem=t_recv.at[s - 1, h, t, 1],
            device_id=at_col(-s),
            device_id_type=MESH,
        )

    loads[0].wait()

    def turn(p, carry):
        turned = b_raw[p].T
        for h in range(HALVES):
            b_held[0][h][p] = turned[h * strip : (h + 1) * strip, :]
        return carry

    lax.fori_loop(0, pad_b, turn, 0, unroll=True)
    loads[1].wait()
    loads[2].wait()
    codes[0] = jnp.full((8, 128), -1, jnp.int32)
    codes[0, 0:1, 0:pad_b] = slot_codes(b_rows, b_cols, b_count, CB)

    pl.semaphore_wait(barrier, jnp.where(at_first, STEPS + 2, STEPS))
    code_hop(0).start()
    for h in range(HALVES):
        start_half(0, h)

    loads[3].wait()
    loads[4].wait()
    found_a[...] = slot_of_block(slot_codes(a_rows, a_cols, a_count, KB), RB * KB, pad_a)
    a_table = pltpu.make_async_copy(found_a, where_a, table_sem.at[STEPS])
    a_table.start()

    def b_table(s):
        return pltpu.make_async_copy(found_b.at[s], where_b.at[s], table_sem.at[s])

    def find_b(s):
        found_b[s] = slot_of_block(codes[s, 0:1, :], KB * CB, pad_b)
        b_table(s).start()

    find_b(0)
    a_table.wait()
    loads[5].wait()

    def place_a(p, carry):
        r, c = p // KB, p % KB
        a_dense[
            pl.ds(pl.multiple_of(r * bs, bs), bs), pl.ds(pl.multiple_of(c * bs, bs), bs)
        ] = a_held[where_a[p, 0]]
        return carry

    lax.fori_loop(0, RB * KB, place_a, 0, unroll=8)

    def place_b(s, h):
        def place(r, carry):
            for c in range(CB):
                b_dense[
                    h, c * strip : (c + 1) * strip, pl.ds(pl.multiple_of(r * bs, bs), bs)
                ] = b_held[s][h][where_b[s, r * CB + c, 0]]
            return carry

        lax.fori_loop(0, KB, place, 0, unroll=4)

    def product(h, t):
        return lax.dot_general(
            a_dense[tile_rows(t), :],
            b_dense[h],
            (((1,), (1,)), ((), ())),
            preferred_element_type=jnp.float32,
        )

    def own_tile(h, t, carry):
        total[h, tile_rows(t), :] = product(h, t)
        return carry

    def sent_tile(s, h, t, carry):
        term = product(h, t)
        largest = jnp.maximum(jnp.max(jnp.abs(term), axis=0, keepdims=True), 1e-30)
        scale_out[s - 1, h, t] = largest * (1.0 / 32767.0)
        scale_home(s, h, t).start()
        coded = jnp.round(term * (32767.0 / largest))
        t_out[s - 1, h, tile_rows(t), :] = coded.astype(jnp.int32).astype(jnp.int16)
        tile_home(s, h, t).start()
        return carry

    def term_from(s, h, t):
        scale_home(s, h, t).wait_recv()
        tile_home(s, h, t).wait_recv()
        return t_in[s - 1, h, tile_rows(t), :].astype(jnp.float32) * scale_in[s - 1, h, t]

    def add_tile(s, h, t, carry):
        total[h, tile_rows(t), :] = total[h, tile_rows(t), :] + term_from(s, h, t)
        return carry

    b_table(0).wait()
    for h in range(HALVES):
        place_b(0, h)
        lax.fori_loop(0, TILES, functools.partial(own_tile, h), 0)

    for s in range(1, STEPS):
        start_pass(s - 1)
        code_hop(s - 1).wait_recv()
        if s < STEPS - 1:
            code_hop(s).start()
        find_b(s)
        b_table(s).wait()
        for h in range(HALVES):
            half_hop(s - 1, h).wait_recv()
            if s < STEPS - 1:
                start_half(s, h)
            place_b(s, h)
            lax.fori_loop(0, TILES, functools.partial(sent_tile, s, h), 0)

    for s in range(1, STEPS):
        for h in range(HALVES):
            lax.fori_loop(0, TILES, functools.partial(add_tile, s, h), 0)

    def finish(t, carry):
        for c in range(CB):
            strips = [total[h, tile_rows(t), c * strip : (c + 1) * strip] for h in range(HALVES)]
            out_ref[tile_rows(t), c * bs : (c + 1) * bs] = jnp.concatenate(strips, axis=1).astype(jnp.bfloat16)
        return carry

    lax.fori_loop(0, TILES, finish, 0)

    @pl.when(at_first)
    def _():
        for s in range(STEPS - 1):
            pass_on(s).wait_send()

    for s in range(STEPS - 1):
        code_hop(s).wait_send()
        for h in range(HALVES):
            half_hop(s, h).wait_send()
            for t in range(TILES):
                tile_home(s + 1, h, t).wait_send()
                scale_home(s + 1, h, t).wait_send()


def per_device(a_blocks, a_rows, a_cols, a_count, b_blocks, b_rows, b_cols, b_count):
    grid_rows, grid_cols = lax.axis_size("row"), lax.axis_size("col")
    pad_a, bs = a_blocks.shape[2], a_blocks.shape[3]
    pad_b = b_blocks.shape[2]
    vmem = pl.BlockSpec(memory_space=pltpu.VMEM)
    smem = pl.BlockSpec(memory_space=pltpu.SMEM)
    whole = pl.BlockSpec(memory_space=pltpu.HBM)
    rows, depth, columns = RB * bs, KB * bs, CB * bs
    strip, wide = bs // HALVES, columns // HALVES
    return pl.pallas_call(
        functools.partial(kernel, grid_rows, grid_cols),
        out_shape=jax.ShapeDtypeStruct((rows, columns), jnp.bfloat16),
        in_specs=[whole, whole, smem, whole, whole, smem, whole, whole],
        out_specs=vmem,
        scratch_shapes=[
            pltpu.VMEM((1, pad_a), jnp.int32),
            pltpu.VMEM((1, pad_a), jnp.int32),
            pltpu.VMEM((1, pad_b), jnp.int32),
            pltpu.VMEM((1, pad_b), jnp.int32),
            pltpu.VMEM((pad_a + 1, bs, bs), jnp.bfloat16),
            pltpu.VMEM((rows, depth), jnp.bfloat16),
            pltpu.VMEM((pad_b, bs, bs), jnp.bfloat16),
            *[pltpu.VMEM((pad_b + 1, strip, bs), jnp.bfloat16)] * (STEPS * HALVES),
            pltpu.VMEM((HALVES, wide, depth), jnp.bfloat16),
            pltpu.VMEM((STEPS, 8, 128), jnp.int32),
            pltpu.VMEM((RB * KB, 128), jnp.int32),
            pltpu.VMEM((STEPS, KB * CB, 128), jnp.int32),
            pltpu.SMEM((RB * KB, 128), jnp.int32),
            pltpu.SMEM((STEPS, KB * CB, 128), jnp.int32),
            pltpu.VMEM((HALVES, rows, wide), jnp.float32),
            pltpu.VMEM((STEPS - 1, HALVES, rows, wide), jnp.int16),
            pltpu.VMEM((STEPS - 1, HALVES, rows, wide), jnp.int16),
            pltpu.VMEM((STEPS - 1, HALVES, TILES, 1, wide), jnp.float32),
            pltpu.VMEM((STEPS - 1, HALVES, TILES, 1, wide), jnp.float32),
            pltpu.VMEM((STEPS - 1, pad_b, strip, bs), jnp.bfloat16),
            pltpu.SemaphoreType.DMA((6,)),
            pltpu.SemaphoreType.DMA((STEPS + 1,)),
            pltpu.SemaphoreType.DMA((STEPS - 1, HALVES + 1)),
            pltpu.SemaphoreType.DMA((STEPS - 1, HALVES + 1)),
            pltpu.SemaphoreType.DMA((STEPS - 1,)),
            pltpu.SemaphoreType.DMA((STEPS - 1,)),
            pltpu.SemaphoreType.DMA((STEPS - 1, HALVES, TILES, 2)),
            pltpu.SemaphoreType.DMA((STEPS - 1, HALVES, TILES, 2)),
        ],
        compiler_params=pltpu.CompilerParams(
            collective_id=0, has_side_effects=True, vmem_limit_bytes=60 * 1024 * 1024
        ),
    )(
        a_rows.reshape(1, pad_a),
        a_cols.reshape(1, pad_a),
        a_count,
        b_rows.reshape(1, pad_b),
        b_cols.reshape(1, pad_b),
        b_count,
        a_blocks.reshape(pad_a, bs, bs),
        b_blocks.reshape(pad_b, bs, bs),
    )


def solution(mesh):
    placed = (
        P("row", "col", None, None, None),
        P("row", "col", None),
        P("row", "col", None),
        P("row", "col"),
        P("row", "col", None, None, None),
        P("row", "col", None),
        P("row", "col", None),
        P("row", "col"),
    )
    return jax.shard_map(
        per_device, mesh=mesh, in_specs=placed, out_specs=P("row", "col"), check_vma=False
    )
```

```python
import functools

import jax
import jax.numpy as jnp
from jax import lax
from jax.experimental import pallas as pl
from jax.experimental.pallas import tpu as pltpu
from jax.sharding import PartitionSpec as P

RB = 8
KB = 16
CB = 2
STEPS = 4
HALVES = 2
TILES = 2

MESH = pl.DeviceIdType.MESH


def slot_codes(rows_ref, cols_ref, count_ref, block_cols):
    slots = lax.broadcasted_iota(jnp.int32, rows_ref.shape, 1)
    codes = rows_ref[...] * block_cols + cols_ref[...]
    return jnp.where(slots < count_ref[0, 0], codes, -1)


def slot_of_block(codes, blocks, empty):
    width = codes.shape[1]
    wanted = lax.broadcasted_iota(jnp.int32, (blocks, width), 0)
    slots = lax.broadcasted_iota(jnp.int32, (blocks, width), 1)
    hits = jnp.where(jnp.broadcast_to(codes, (blocks, width)) == wanted, slots, empty)
    return jnp.broadcast_to(jnp.min(hits, axis=1, keepdims=True), (blocks, 128))


def kernel(
    grid_rows,
    grid_cols,
    a_rows_hbm,
    a_cols_hbm,
    a_count,
    b_rows_hbm,
    b_cols_hbm,
    b_count,
    a_blocks,
    b_blocks,
    out_ref,
    a_rows,
    a_cols,
    b_rows,
    b_cols,
    a_held,
    a_dense,
    b_raw,
    own_0,
    own_1,
    one_0,
    one_1,
    two_0,
    two_1,
    three_0,
    three_1,
    b_dense,
    codes,
    found_a,
    found_b,
    where_a,
    where_b,
    total,
    t_out,
    t_in,
    scale_out,
    scale_in,
    passed,
    local_sem,
    table_sem,
    b_send,
    b_recv,
    pass_send,
    pass_recv,
    term_held,
    term_scale,
    term_send,
    term_recv,
    t_send,
    t_recv,
):
    pad_a, bs = a_blocks.shape[0], a_blocks.shape[1]
    pad_b = b_blocks.shape[0]
    strip = bs // HALVES
    tile = RB * bs // TILES
    b_held = ((own_0, own_1), (one_0, one_1), (two_0, two_1), (three_0, three_1))
    i, k = lax.axis_index("row"), lax.axis_index("col")

    def at_col(distance):
        return (i, lax.rem(k + distance + grid_cols, grid_cols))

    onward = (lax.rem(i + grid_rows - 1, grid_rows), lax.rem(k + 1, grid_cols))
    origin = (lax.rem(i + 1, grid_rows), lax.rem(k + grid_cols - 1, grid_cols))

    run, lane = grid_rows // 2, grid_cols // 2

    def passing(row, col):
        return jnp.logical_and(lax.rem(row, run) == 0, lax.rem(col, lane) < lane - 2)

    beside = (lax.rem(i + run, grid_rows), k)
    past_beside = (lax.rem(i + run + grid_rows - 1, grid_rows), lax.rem(k + 1, grid_cols))
    passes_here = (lax.rem(i + 1 + run, grid_rows), lax.rem(k + grid_cols - 1, grid_cols))
    at_first, at_last = passing(i, k), passing(*passes_here)

    nothing = jnp.zeros((strip, bs), jnp.bfloat16)
    for held in b_held:
        for h in range(HALVES):
            held[h][pad_b] = nothing
    a_held[pad_a] = jnp.zeros((bs, bs), jnp.bfloat16)

    barrier = pltpu.get_barrier_semaphore()
    pl.semaphore_signal(barrier, inc=1, device_id=origin, device_id_type=MESH)
    first_y, last_y = lax.rem(k, lane) < 2, lax.rem(k, lane) >= lane - 2
    for distance in (1, jnp.where(last_y, lane, 2), 3):
        pl.semaphore_signal(barrier, inc=1, device_id=at_col(distance), device_id_type=MESH)

    @pl.when(last_y)
    def _():
        pl.semaphore_signal(barrier, inc=1, device_id=at_col(2 + lane), device_id_type=MESH)

    @pl.when(at_last)
    def _():
        pl.semaphore_signal(barrier, inc=1, device_id=passes_here, device_id_type=MESH)

    @pl.when(at_first)
    def _():
        pl.semaphore_signal(barrier, inc=1, device_id=beside, device_id_type=MESH)

    loads = [
        pltpu.make_async_copy(source, target, local_sem.at[n])
        for n, (source, target) in enumerate(
            (
                (b_blocks, b_raw),
                (b_rows_hbm, b_rows),
                (b_cols_hbm, b_cols),
                (a_rows_hbm, a_rows),
                (a_cols_hbm, a_cols),
                (a_blocks, a_held.at[pl.ds(0, pad_a)]),
            )
        )
    ]
    for load in loads:
        load.start()

    def code_hop(s):
        return pltpu.make_async_remote_copy(
            src_ref=codes.at[s],
            dst_ref=codes.at[s + 1],
            send_sem=b_send.at[s, HALVES],
            recv_sem=b_recv.at[s, HALVES],
            device_id=onward,
            device_id_type=MESH,
        )

    def half_hop(s, h):
        return pltpu.make_async_remote_copy(
            src_ref=b_held[s][h].at[pl.ds(0, pad_b)],
            dst_ref=b_held[s + 1][h].at[pl.ds(0, pad_b)],
            send_sem=b_send.at[s, h],
            recv_sem=b_recv.at[s, h],
            device_id=onward,
            device_id_type=MESH,
        )

    def hop_beside(s):
        return pltpu.make_async_remote_copy(
            src_ref=b_held[s][0].at[pl.ds(0, pad_b)],
            dst_ref=passed.at[s],
            send_sem=b_send.at[s, 0],
            recv_sem=pass_recv.at[s],
            device_id=beside,
            device_id_type=MESH,
        )

    def pass_on(s):
        return pltpu.make_async_remote_copy(
            src_ref=passed.at[s],
            dst_ref=b_held[s + 1][0].at[pl.ds(0, pad_b)],
            send_sem=pass_send.at[s],
            recv_sem=b_recv.at[s, 0],
            device_id=past_beside,
            device_id_type=MESH,
        )

    def start_half(s, h):
        if h > 0:
            half_hop(s, h).start()
            return

        @pl.when(at_first)
        def _():
            hop_beside(s).start()

        @pl.when(jnp.logical_not(at_first))
        def _():
            half_hop(s, h).start()

    def start_pass(s):
        @pl.when(at_first)
        def _():
            hop_beside(s).wait_recv()
            pass_on(s).start()

    def tile_rows(t):
        return pl.ds(pl.multiple_of(t * tile, tile), tile)

    def tile_home(s, h, t):
        return pltpu.make_async_remote_copy(
            src_ref=t_out.at[s - 1, h, tile_rows(t)],
            dst_ref=t_in.at[s - 1, h, tile_rows(t)],
            send_sem=t_send.at[s - 1, h, t, 0],
            recv_sem=t_recv.at[s - 1, h, t, 0],
            device_id=at_col(-s),
            device_id_type=MESH,
        )

    def scale_home(s, h, t):
        return pltpu.make_async_remote_copy(
            src_ref=scale_out.at[s - 1, h, t],
            dst_ref=scale_in.at[s - 1, h, t],
            send_sem=t_send.at[s - 1, h, t, 1],
            recv_sem=t_recv.at[s - 1, h, t, 1],
            device_id=at_col(-s),
            device_id_type=MESH,
        )

    def beside_home(h, t):
        return (
            pltpu.make_async_remote_copy(
                src_ref=t_out.at[1, h, tile_rows(t)],
                dst_ref=term_held.at[h, tile_rows(t)],
                send_sem=t_send.at[1, h, t, 0],
                recv_sem=term_recv.at[h, t, 0],
                device_id=at_col(lane - 2),
                device_id_type=MESH,
            ),
            pltpu.make_async_remote_copy(
                src_ref=scale_out.at[1, h, t],
                dst_ref=term_scale.at[h, t],
                send_sem=t_send.at[1, h, t, 1],
                recv_sem=term_recv.at[h, t, 1],
                device_id=at_col(lane - 2),
                device_id_type=MESH,
            ),
        )

    def passed_home(h, t):
        return (
            pltpu.make_async_remote_copy(
                src_ref=term_held.at[h, tile_rows(t)],
                dst_ref=t_in.at[1, h, tile_rows(t)],
                send_sem=term_send.at[h, t, 0],
                recv_sem=t_recv.at[1, h, t, 0],
                device_id=at_col(lane),
                device_id_type=MESH,
            ),
            pltpu.make_async_remote_copy(
                src_ref=term_scale.at[h, t],
                dst_ref=scale_in.at[1, h, t],
                send_sem=term_send.at[h, t, 1],
                recv_sem=t_recv.at[1, h, t, 1],
                device_id=at_col(lane),
                device_id_type=MESH,
            ),
        )

    def start_home(s, h, t):
        def straight():
            scale_home(s, h, t).start()
            tile_home(s, h, t).start()

        if s != 2:
            straight()
            return

        @pl.when(first_y)
        def _():
            for copy in beside_home(h, t):
                copy.start()

        pl.when(jnp.logical_not(first_y))(straight)

    def pass_home(h):
        @pl.when(last_y)
        def _():
            for t in range(TILES):
                for copy in beside_home(h, t):
                    copy.wait_recv()
                for copy in passed_home(h, t):
                    copy.start()

    loads[0].wait()

    def turn(p, carry):
        turned = b_raw[p].T
        for h in range(HALVES):
            b_held[0][h][p] = turned[h * strip : (h + 1) * strip, :]
        return carry

    lax.fori_loop(0, pad_b, turn, 0, unroll=True)
    loads[1].wait()
    loads[2].wait()
    codes[0] = jnp.full((8, 128), -1, jnp.int32)
    codes[0, 0:1, 0:pad_b] = slot_codes(b_rows, b_cols, b_count, CB)

    pl.semaphore_wait(barrier, STEPS + jnp.where(at_first, 2, 0) + jnp.where(last_y, 1, 0))
    code_hop(0).start()
    for h in range(HALVES):
        start_half(0, h)

    loads[3].wait()
    loads[4].wait()
    found_a[...] = slot_of_block(slot_codes(a_rows, a_cols, a_count, KB), RB * KB, pad_a)
    a_table = pltpu.make_async_copy(found_a, where_a, table_sem.at[STEPS])
    a_table.start()

    def b_table(s):
        return pltpu.make_async_copy(found_b.at[s], where_b.at[s], table_sem.at[s])

    def find_b(s):
        found_b[s] = slot_of_block(codes[s, 0:1, :], KB * CB, pad_b)
        b_table(s).start()

    find_b(0)
    a_table.wait()
    loads[5].wait()

    def place_a(p, carry):
        r, c = p // KB, p % KB
        a_dense[
            pl.ds(pl.multiple_of(r * bs, bs), bs), pl.ds(pl.multiple_of(c * bs, bs), bs)
        ] = a_held[where_a[p, 0]]
        return carry

    lax.fori_loop(0, RB * KB, place_a, 0, unroll=8)

    def place_b(s, h):
        def place(r, carry):
            for c in range(CB):
                b_dense[
                    h, c * strip : (c + 1) * strip, pl.ds(pl.multiple_of(r * bs, bs), bs)
                ] = b_held[s][h][where_b[s, r * CB + c, 0]]
            return carry

        lax.fori_loop(0, KB, place, 0, unroll=4)

    def product(h, t):
        return lax.dot_general(
            a_dense[tile_rows(t), :],
            b_dense[h],
            (((1,), (1,)), ((), ())),
            preferred_element_type=jnp.float32,
        )

    def own_tile(h, t, carry):
        total[h, tile_rows(t), :] = product(h, t)
        return carry

    def sent_tile(s, h, t, carry):
        term = product(h, t)
        largest = jnp.maximum(jnp.max(jnp.abs(term), axis=0, keepdims=True), 1e-30)
        scale_out[s - 1, h, t] = largest * (1.0 / 32767.0)
        coded = jnp.round(term * (32767.0 / largest))
        t_out[s - 1, h, tile_rows(t), :] = coded.astype(jnp.int32).astype(jnp.int16)
        start_home(s, h, t)
        return carry

    def term_from(s, h, t):
        scale_home(s, h, t).wait_recv()
        tile_home(s, h, t).wait_recv()
        return t_in[s - 1, h, tile_rows(t), :].astype(jnp.float32) * scale_in[s - 1, h, t]

    def add_tile(s, h, t, carry):
        total[h, tile_rows(t), :] = total[h, tile_rows(t), :] + term_from(s, h, t)
        return carry

    b_table(0).wait()
    for h in range(HALVES):
        place_b(0, h)
        lax.fori_loop(0, TILES, functools.partial(own_tile, h), 0)

    start_pass(0)
    for s in range(1, STEPS):
        code_hop(s - 1).wait_recv()
        if s < STEPS - 1:
            code_hop(s).start()
        find_b(s)
        b_table(s).wait()
        for h in range(HALVES):
            half_hop(s - 1, h).wait_recv()
            if s < STEPS - 1:
                start_half(s, h)
            place_b(s, h)
            lax.fori_loop(0, TILES, functools.partial(sent_tile, s, h), 0)
            if s < STEPS - 1 and h == 0:
                start_pass(s)
            if s == STEPS - 1:
                pass_home(h)

    for s in range(1, STEPS):
        for h in range(HALVES):
            lax.fori_loop(0, TILES, functools.partial(add_tile, s, h), 0)

    def finish(t, carry):
        for c in range(CB):
            strips = [total[h, tile_rows(t), c * strip : (c + 1) * strip] for h in range(HALVES)]
            out_ref[tile_rows(t), c * bs : (c + 1) * bs] = jnp.concatenate(strips, axis=1).astype(jnp.bfloat16)
        return carry

    lax.fori_loop(0, TILES, finish, 0)

    @pl.when(at_first)
    def _():
        for s in range(STEPS - 1):
            pass_on(s).wait_send()

    @pl.when(last_y)
    def _():
        for h in range(HALVES):
            for t in range(TILES):
                for copy in passed_home(h, t):
                    copy.wait_send()

    for s in range(STEPS - 1):
        code_hop(s).wait_send()
        for h in range(HALVES):
            half_hop(s, h).wait_send()
            for t in range(TILES):
                tile_home(s + 1, h, t).wait_send()
                scale_home(s + 1, h, t).wait_send()


def per_device(a_blocks, a_rows, a_cols, a_count, b_blocks, b_rows, b_cols, b_count):
    grid_rows, grid_cols = lax.axis_size("row"), lax.axis_size("col")
    pad_a, bs = a_blocks.shape[2], a_blocks.shape[3]
    pad_b = b_blocks.shape[2]
    vmem = pl.BlockSpec(memory_space=pltpu.VMEM)
    smem = pl.BlockSpec(memory_space=pltpu.SMEM)
    whole = pl.BlockSpec(memory_space=pltpu.HBM)
    rows, depth, columns = RB * bs, KB * bs, CB * bs
    strip, wide = bs // HALVES, columns // HALVES
    return pl.pallas_call(
        functools.partial(kernel, grid_rows, grid_cols),
        out_shape=jax.ShapeDtypeStruct((rows, columns), jnp.bfloat16),
        in_specs=[whole, whole, smem, whole, whole, smem, whole, whole],
        out_specs=vmem,
        scratch_shapes=[
            pltpu.VMEM((1, pad_a), jnp.int32),
            pltpu.VMEM((1, pad_a), jnp.int32),
            pltpu.VMEM((1, pad_b), jnp.int32),
            pltpu.VMEM((1, pad_b), jnp.int32),
            pltpu.VMEM((pad_a + 1, bs, bs), jnp.bfloat16),
            pltpu.VMEM((rows, depth), jnp.bfloat16),
            pltpu.VMEM((pad_b, bs, bs), jnp.bfloat16),
            *[pltpu.VMEM((pad_b + 1, strip, bs), jnp.bfloat16)] * (STEPS * HALVES),
            pltpu.VMEM((HALVES, wide, depth), jnp.bfloat16),
            pltpu.VMEM((STEPS, 8, 128), jnp.int32),
            pltpu.VMEM((RB * KB, 128), jnp.int32),
            pltpu.VMEM((STEPS, KB * CB, 128), jnp.int32),
            pltpu.SMEM((RB * KB, 128), jnp.int32),
            pltpu.SMEM((STEPS, KB * CB, 128), jnp.int32),
            pltpu.VMEM((HALVES, rows, wide), jnp.float32),
            pltpu.VMEM((STEPS - 1, HALVES, rows, wide), jnp.int16),
            pltpu.VMEM((STEPS - 1, HALVES, rows, wide), jnp.int16),
            pltpu.VMEM((STEPS - 1, HALVES, TILES, 1, wide), jnp.float32),
            pltpu.VMEM((STEPS - 1, HALVES, TILES, 1, wide), jnp.float32),
            pltpu.VMEM((STEPS - 1, pad_b, strip, bs), jnp.bfloat16),
            pltpu.SemaphoreType.DMA((6,)),
            pltpu.SemaphoreType.DMA((STEPS + 1,)),
            pltpu.SemaphoreType.DMA((STEPS - 1, HALVES + 1)),
            pltpu.SemaphoreType.DMA((STEPS - 1, HALVES + 1)),
            pltpu.SemaphoreType.DMA((STEPS - 1,)),
            pltpu.SemaphoreType.DMA((STEPS - 1,)),
            pltpu.VMEM((HALVES, rows, wide), jnp.int16),
            pltpu.VMEM((HALVES, TILES, 1, wide), jnp.float32),
            pltpu.SemaphoreType.DMA((HALVES, TILES, 2)),
            pltpu.SemaphoreType.DMA((HALVES, TILES, 2)),
            pltpu.SemaphoreType.DMA((STEPS - 1, HALVES, TILES, 2)),
            pltpu.SemaphoreType.DMA((STEPS - 1, HALVES, TILES, 2)),
        ],
        compiler_params=pltpu.CompilerParams(
            collective_id=0, has_side_effects=True, vmem_limit_bytes=60 * 1024 * 1024
        ),
    )(
        a_rows.reshape(1, pad_a),
        a_cols.reshape(1, pad_a),
        a_count,
        b_rows.reshape(1, pad_b),
        b_cols.reshape(1, pad_b),
        b_count,
        a_blocks.reshape(pad_a, bs, bs),
        b_blocks.reshape(pad_b, bs, bs),
    )


def solution(mesh):
    placed = (
        P("row", "col", None, None, None),
        P("row", "col", None),
        P("row", "col", None),
        P("row", "col"),
        P("row", "col", None, None, None),
        P("row", "col", None),
        P("row", "col", None),
        P("row", "col"),
    )
    return jax.shard_map(
        per_device, mesh=mesh, in_specs=placed, out_specs=P("row", "col"), check_vma=False
    )
```

```python
import functools

import jax
import jax.numpy as jnp
from jax import lax
from jax.experimental import pallas as pl
from jax.experimental.pallas import tpu as pltpu
from jax.sharding import PartitionSpec as P

RB = 8
KB = 16
CB = 2
STEPS = 4
HALVES = 2
TILES = 2

MESH = pl.DeviceIdType.MESH


def slot_codes(rows_ref, cols_ref, count_ref, block_cols):
    slots = lax.broadcasted_iota(jnp.int32, rows_ref.shape, 1)
    codes = rows_ref[...] * block_cols + cols_ref[...]
    return jnp.where(slots < count_ref[0, 0], codes, -1)


def slot_of_block(codes, blocks, empty):
    width = codes.shape[1]
    wanted = lax.broadcasted_iota(jnp.int32, (blocks, width), 0)
    slots = lax.broadcasted_iota(jnp.int32, (blocks, width), 1)
    hits = jnp.where(jnp.broadcast_to(codes, (blocks, width)) == wanted, slots, empty)
    return jnp.broadcast_to(jnp.min(hits, axis=1, keepdims=True), (blocks, 128))


def kernel(
    grid_rows,
    grid_cols,
    a_rows_hbm,
    a_cols_hbm,
    a_count,
    b_rows_hbm,
    b_cols_hbm,
    b_count,
    a_blocks,
    b_blocks,
    out_ref,
    a_rows,
    a_cols,
    b_rows,
    b_cols,
    a_held,
    a_dense,
    b_raw,
    own_0,
    own_1,
    one_0,
    one_1,
    two_0,
    two_1,
    three_0,
    three_1,
    b_dense,
    codes,
    found_a,
    found_b,
    where_a,
    where_b,
    total,
    t_out,
    t_in,
    scale_out,
    scale_in,
    passed,
    local_sem,
    table_sem,
    b_send,
    b_recv,
    pass_send,
    pass_recv,
    term_held,
    term_scale,
    term_send,
    term_recv,
    t_send,
    t_recv,
):
    pad_a, bs = a_blocks.shape[0], a_blocks.shape[1]
    pad_b = b_blocks.shape[0]
    strip = bs // HALVES
    tile = RB * bs // TILES
    b_held = ((own_0, own_1), (one_0, one_1), (two_0, two_1), (three_0, three_1))
    i, k = lax.axis_index("row"), lax.axis_index("col")

    def at_col(distance):
        return (i, lax.rem(k + distance + grid_cols, grid_cols))

    onward = (lax.rem(i + grid_rows - 1, grid_rows), lax.rem(k + 1, grid_cols))
    origin = (lax.rem(i + 1, grid_rows), lax.rem(k + grid_cols - 1, grid_cols))

    run, lane = grid_rows // 2, grid_cols // 2

    def passing(row, col):
        return jnp.logical_and(lax.rem(row, run) == 0, lax.rem(col, lane) < lane - 2)

    beside = (lax.rem(i + run, grid_rows), k)
    past_beside = (lax.rem(i + run + grid_rows - 1, grid_rows), lax.rem(k + 1, grid_cols))
    passes_here = (lax.rem(i + 1 + run, grid_rows), lax.rem(k + grid_cols - 1, grid_cols))
    at_first, at_last = passing(i, k), passing(*passes_here)

    nothing = jnp.zeros((strip, bs), jnp.bfloat16)
    for held in b_held:
        for h in range(HALVES):
            held[h][pad_b] = nothing
    a_held[pad_a] = jnp.zeros((bs, bs), jnp.bfloat16)

    barrier = pltpu.get_barrier_semaphore()
    pl.semaphore_signal(barrier, inc=1, device_id=origin, device_id_type=MESH)
    first_y, last_y = lax.rem(k, lane) < 2, lax.rem(k, lane) >= lane - 2
    for distance in (1, jnp.where(last_y, lane, 2), 3):
        pl.semaphore_signal(barrier, inc=1, device_id=at_col(distance), device_id_type=MESH)

    @pl.when(last_y)
    def _():
        pl.semaphore_signal(barrier, inc=1, device_id=at_col(2 + lane), device_id_type=MESH)

    @pl.when(at_last)
    def _():
        pl.semaphore_signal(barrier, inc=1, device_id=passes_here, device_id_type=MESH)

    @pl.when(at_first)
    def _():
        pl.semaphore_signal(barrier, inc=1, device_id=beside, device_id_type=MESH)

    loads = [
        pltpu.make_async_copy(source, target, local_sem.at[n])
        for n, (source, target) in enumerate(
            (
                (b_blocks, b_raw),
                (b_rows_hbm, b_rows),
                (b_cols_hbm, b_cols),
                (a_rows_hbm, a_rows),
                (a_cols_hbm, a_cols),
                (a_blocks, a_held.at[pl.ds(0, pad_a)]),
            )
        )
    ]
    for load in loads:
        load.start()

    def code_hop(s):
        return pltpu.make_async_remote_copy(
            src_ref=codes.at[s],
            dst_ref=codes.at[s + 1],
            send_sem=b_send.at[s, HALVES],
            recv_sem=b_recv.at[s, HALVES],
            device_id=onward,
            device_id_type=MESH,
        )

    def half_hop(s, h):
        return pltpu.make_async_remote_copy(
            src_ref=b_held[s][h].at[pl.ds(0, pad_b)],
            dst_ref=b_held[s + 1][h].at[pl.ds(0, pad_b)],
            send_sem=b_send.at[s, h],
            recv_sem=b_recv.at[s, h],
            device_id=onward,
            device_id_type=MESH,
        )

    def hop_beside(s):
        return pltpu.make_async_remote_copy(
            src_ref=b_held[s][1].at[pl.ds(0, pad_b)],
            dst_ref=passed.at[s],
            send_sem=b_send.at[s, 1],
            recv_sem=pass_recv.at[s],
            device_id=beside,
            device_id_type=MESH,
        )

    def pass_on(s):
        return pltpu.make_async_remote_copy(
            src_ref=passed.at[s],
            dst_ref=b_held[s + 1][1].at[pl.ds(0, pad_b)],
            send_sem=pass_send.at[s],
            recv_sem=b_recv.at[s, 1],
            device_id=past_beside,
            device_id_type=MESH,
        )

    def start_half(s, h):
        if h < HALVES - 1:
            half_hop(s, h).start()
            return

        @pl.when(at_first)
        def _():
            hop_beside(s).start()

        @pl.when(jnp.logical_not(at_first))
        def _():
            half_hop(s, h).start()

    def start_pass(s):
        @pl.when(at_first)
        def _():
            hop_beside(s).wait_recv()
            pass_on(s).start()

    def tile_rows(t):
        return pl.ds(pl.multiple_of(t * tile, tile), tile)

    def tile_home(s, h, t):
        return pltpu.make_async_remote_copy(
            src_ref=t_out.at[s - 1, h, tile_rows(t)],
            dst_ref=t_in.at[s - 1, h, tile_rows(t)],
            send_sem=t_send.at[s - 1, h, t, 0],
            recv_sem=t_recv.at[s - 1, h, t, 0],
            device_id=at_col(-s),
            device_id_type=MESH,
        )

    def scale_home(s, h, t):
        return pltpu.make_async_remote_copy(
            src_ref=scale_out.at[s - 1, h, t],
            dst_ref=scale_in.at[s - 1, h, t],
            send_sem=t_send.at[s - 1, h, t, 1],
            recv_sem=t_recv.at[s - 1, h, t, 1],
            device_id=at_col(-s),
            device_id_type=MESH,
        )

    def beside_home(h, t):
        return (
            pltpu.make_async_remote_copy(
                src_ref=t_out.at[1, h, tile_rows(t)],
                dst_ref=term_held.at[h, tile_rows(t)],
                send_sem=t_send.at[1, h, t, 0],
                recv_sem=term_recv.at[h, t, 0],
                device_id=at_col(lane - 2),
                device_id_type=MESH,
            ),
            pltpu.make_async_remote_copy(
                src_ref=scale_out.at[1, h, t],
                dst_ref=term_scale.at[h, t],
                send_sem=t_send.at[1, h, t, 1],
                recv_sem=term_recv.at[h, t, 1],
                device_id=at_col(lane - 2),
                device_id_type=MESH,
            ),
        )

    def passed_home(h, t):
        return (
            pltpu.make_async_remote_copy(
                src_ref=term_held.at[h, tile_rows(t)],
                dst_ref=t_in.at[1, h, tile_rows(t)],
                send_sem=term_send.at[h, t, 0],
                recv_sem=t_recv.at[1, h, t, 0],
                device_id=at_col(lane),
                device_id_type=MESH,
            ),
            pltpu.make_async_remote_copy(
                src_ref=term_scale.at[h, t],
                dst_ref=scale_in.at[1, h, t],
                send_sem=term_send.at[h, t, 1],
                recv_sem=t_recv.at[1, h, t, 1],
                device_id=at_col(lane),
                device_id_type=MESH,
            ),
        )

    def start_home(s, h, t):
        def straight():
            scale_home(s, h, t).start()
            tile_home(s, h, t).start()

        if s != 2:
            straight()
            return

        @pl.when(first_y)
        def _():
            for copy in beside_home(h, t):
                copy.start()

        pl.when(jnp.logical_not(first_y))(straight)

    def pass_home(h):
        @pl.when(last_y)
        def _():
            for t in range(TILES):
                for copy in beside_home(h, t):
                    copy.wait_recv()
                for copy in passed_home(h, t):
                    copy.start()

    loads[0].wait()

    def turn(h):
        def turn_block(p, carry):
            b_held[0][h][p] = b_raw[p, :, h * strip : (h + 1) * strip].T
            return carry

        lax.fori_loop(0, pad_b, turn_block, 0, unroll=True)

    turn(0)
    loads[1].wait()
    loads[2].wait()
    codes[0] = jnp.full((8, 128), -1, jnp.int32)
    codes[0, 0:1, 0:pad_b] = slot_codes(b_rows, b_cols, b_count, CB)

    pl.semaphore_wait(barrier, STEPS + jnp.where(at_first, 2, 0) + jnp.where(last_y, 1, 0))
    code_hop(0).start()
    start_half(0, 0)
    for h in range(1, HALVES):
        turn(h)
        start_half(0, h)

    loads[3].wait()
    loads[4].wait()
    found_a[...] = slot_of_block(slot_codes(a_rows, a_cols, a_count, KB), RB * KB, pad_a)
    a_table = pltpu.make_async_copy(found_a, where_a, table_sem.at[STEPS])
    a_table.start()

    def b_table(s):
        return pltpu.make_async_copy(found_b.at[s], where_b.at[s], table_sem.at[s])

    def find_b(s):
        found_b[s] = slot_of_block(codes[s, 0:1, :], KB * CB, pad_b)
        b_table(s).start()

    find_b(0)
    a_table.wait()
    loads[5].wait()

    def place_a(p, carry):
        r, c = p // KB, p % KB
        a_dense[
            pl.ds(pl.multiple_of(r * bs, bs), bs), pl.ds(pl.multiple_of(c * bs, bs), bs)
        ] = a_held[where_a[p, 0]]
        return carry

    lax.fori_loop(0, RB * KB, place_a, 0, unroll=8)

    def place_b(s, h):
        def place(r, carry):
            for c in range(CB):
                b_dense[
                    h, c * strip : (c + 1) * strip, pl.ds(pl.multiple_of(r * bs, bs), bs)
                ] = b_held[s][h][where_b[s, r * CB + c, 0]]
            return carry

        lax.fori_loop(0, KB, place, 0, unroll=4)

    def product(h, t):
        return lax.dot_general(
            a_dense[tile_rows(t), :],
            b_dense[h],
            (((1,), (1,)), ((), ())),
            preferred_element_type=jnp.float32,
        )

    def own_tile(h, t, carry):
        total[h, tile_rows(t), :] = product(h, t)
        return carry

    def sent_tile(s, h, t, carry):
        term = product(h, t)
        largest = jnp.maximum(jnp.max(jnp.abs(term), axis=0, keepdims=True), 1e-30)
        scale_out[s - 1, h, t] = largest * (1.0 / 32767.0)
        coded = jnp.round(term * (32767.0 / largest))
        t_out[s - 1, h, tile_rows(t), :] = coded.astype(jnp.int32).astype(jnp.int16)
        start_home(s, h, t)
        return carry

    def term_from(s, h, t):
        scale_home(s, h, t).wait_recv()
        tile_home(s, h, t).wait_recv()
        return t_in[s - 1, h, tile_rows(t), :].astype(jnp.float32) * scale_in[s - 1, h, t]

    def add_tile(s, h, t, carry):
        total[h, tile_rows(t), :] = total[h, tile_rows(t), :] + term_from(s, h, t)
        return carry

    b_table(0).wait()
    for h in range(HALVES):
        place_b(0, h)
        lax.fori_loop(0, TILES, functools.partial(own_tile, h), 0)

    start_pass(0)
    for s in range(1, STEPS):
        code_hop(s - 1).wait_recv()
        if s < STEPS - 1:
            code_hop(s).start()
        find_b(s)
        b_table(s).wait()
        for h in range(HALVES):
            half_hop(s - 1, h).wait_recv()
            if s < STEPS - 1:
                start_half(s, h)
            place_b(s, h)
            lax.fori_loop(0, TILES, functools.partial(sent_tile, s, h), 0)
            if s > 1 and h == 0:
                start_pass(s - 1)
            if s == STEPS - 1:
                pass_home(h)

    for s in range(1, STEPS):
        for h in range(HALVES):
            lax.fori_loop(0, TILES, functools.partial(add_tile, s, h), 0)

    def finish(t, carry):
        for c in range(CB):
            strips = [total[h, tile_rows(t), c * strip : (c + 1) * strip] for h in range(HALVES)]
            out_ref[tile_rows(t), c * bs : (c + 1) * bs] = jnp.concatenate(strips, axis=1).astype(jnp.bfloat16)
        return carry

    lax.fori_loop(0, TILES, finish, 0)

    @pl.when(at_first)
    def _():
        for s in range(STEPS - 1):
            pass_on(s).wait_send()

    @pl.when(last_y)
    def _():
        for h in range(HALVES):
            for t in range(TILES):
                for copy in passed_home(h, t):
                    copy.wait_send()

    for s in range(STEPS - 1):
        code_hop(s).wait_send()
        for h in range(HALVES):
            half_hop(s, h).wait_send()
            for t in range(TILES):
                tile_home(s + 1, h, t).wait_send()
                scale_home(s + 1, h, t).wait_send()


def per_device(a_blocks, a_rows, a_cols, a_count, b_blocks, b_rows, b_cols, b_count):
    grid_rows, grid_cols = lax.axis_size("row"), lax.axis_size("col")
    pad_a, bs = a_blocks.shape[2], a_blocks.shape[3]
    pad_b = b_blocks.shape[2]
    vmem = pl.BlockSpec(memory_space=pltpu.VMEM)
    smem = pl.BlockSpec(memory_space=pltpu.SMEM)
    whole = pl.BlockSpec(memory_space=pltpu.HBM)
    rows, depth, columns = RB * bs, KB * bs, CB * bs
    strip, wide = bs // HALVES, columns // HALVES
    return pl.pallas_call(
        functools.partial(kernel, grid_rows, grid_cols),
        out_shape=pltpu.VMEM((rows, columns), jnp.bfloat16),
        in_specs=[whole, whole, smem, whole, whole, smem, whole, whole],
        out_specs=vmem,
        scratch_shapes=[
            pltpu.VMEM((1, pad_a), jnp.int32),
            pltpu.VMEM((1, pad_a), jnp.int32),
            pltpu.VMEM((1, pad_b), jnp.int32),
            pltpu.VMEM((1, pad_b), jnp.int32),
            pltpu.VMEM((pad_a + 1, bs, bs), jnp.bfloat16),
            pltpu.VMEM((rows, depth), jnp.bfloat16),
            pltpu.VMEM((pad_b, bs, bs), jnp.bfloat16),
            *[pltpu.VMEM((pad_b + 1, strip, bs), jnp.bfloat16)] * (STEPS * HALVES),
            pltpu.VMEM((HALVES, wide, depth), jnp.bfloat16),
            pltpu.VMEM((STEPS, 8, 128), jnp.int32),
            pltpu.VMEM((RB * KB, 128), jnp.int32),
            pltpu.VMEM((STEPS, KB * CB, 128), jnp.int32),
            pltpu.SMEM((RB * KB, 128), jnp.int32),
            pltpu.SMEM((STEPS, KB * CB, 128), jnp.int32),
            pltpu.VMEM((HALVES, rows, wide), jnp.float32),
            pltpu.VMEM((STEPS - 1, HALVES, rows, wide), jnp.int16),
            pltpu.VMEM((STEPS - 1, HALVES, rows, wide), jnp.int16),
            pltpu.VMEM((STEPS - 1, HALVES, TILES, 1, wide), jnp.float32),
            pltpu.VMEM((STEPS - 1, HALVES, TILES, 1, wide), jnp.float32),
            pltpu.VMEM((STEPS - 1, pad_b, strip, bs), jnp.bfloat16),
            pltpu.SemaphoreType.DMA((6,)),
            pltpu.SemaphoreType.DMA((STEPS + 1,)),
            pltpu.SemaphoreType.DMA((STEPS - 1, HALVES + 1)),
            pltpu.SemaphoreType.DMA((STEPS - 1, HALVES + 1)),
            pltpu.SemaphoreType.DMA((STEPS - 1,)),
            pltpu.SemaphoreType.DMA((STEPS - 1,)),
            pltpu.VMEM((HALVES, rows, wide), jnp.int16),
            pltpu.VMEM((HALVES, TILES, 1, wide), jnp.float32),
            pltpu.SemaphoreType.DMA((HALVES, TILES, 2)),
            pltpu.SemaphoreType.DMA((HALVES, TILES, 2)),
            pltpu.SemaphoreType.DMA((STEPS - 1, HALVES, TILES, 2)),
            pltpu.SemaphoreType.DMA((STEPS - 1, HALVES, TILES, 2)),
        ],
        compiler_params=pltpu.CompilerParams(
            collective_id=0, has_side_effects=True, vmem_limit_bytes=60 * 1024 * 1024
        ),
    )(
        a_rows.reshape(1, pad_a),
        a_cols.reshape(1, pad_a),
        a_count,
        b_rows.reshape(1, pad_b),
        b_cols.reshape(1, pad_b),
        b_count,
        a_blocks.reshape(pad_a, bs, bs),
        b_blocks.reshape(pad_b, bs, bs),
    )


def solution(mesh):
    placed = (
        P("row", "col", None, None, None),
        P("row", "col", None),
        P("row", "col", None),
        P("row", "col"),
        P("row", "col", None, None, None),
        P("row", "col", None),
        P("row", "col", None),
        P("row", "col"),
    )
    return jax.shard_map(
        per_device, mesh=mesh, in_specs=placed, out_specs=P("row", "col"), check_vma=False
    )
```

```python
import functools

import jax
import jax.numpy as jnp
from jax import lax
from jax.experimental import pallas as pl
from jax.experimental.pallas import tpu as pltpu
from jax.sharding import PartitionSpec as P

RB = 8
KB = 16
CB = 2
STEPS = 4
STRIPS = 4
HALVES = 2
TILES = 2
PER = STRIPS // HALVES

MESH = pl.DeviceIdType.MESH


def slot_codes(rows_ref, cols_ref, count_ref, block_cols):
    slots = lax.broadcasted_iota(jnp.int32, rows_ref.shape, 1)
    codes = rows_ref[...] * block_cols + cols_ref[...]
    return jnp.where(slots < count_ref[...], codes, -1)


def slot_of_block(codes, blocks, empty):
    width = codes.shape[1]
    wanted = lax.broadcasted_iota(jnp.int32, (blocks, width), 0)
    slots = lax.broadcasted_iota(jnp.int32, (blocks, width), 1)
    hits = jnp.where(jnp.broadcast_to(codes, (blocks, width)) == wanted, slots, empty)
    return jnp.broadcast_to(jnp.min(hits, axis=1, keepdims=True), (blocks, 128))


def kernel(
    grid_rows,
    grid_cols,
    a_rows_hbm,
    a_cols_hbm,
    a_count_hbm,
    b_rows_hbm,
    b_cols_hbm,
    b_count_hbm,
    a_blocks,
    b_blocks,
    out_ref,
    a_rows,
    a_cols,
    a_count,
    b_rows,
    b_cols,
    b_count,
    a_held,
    a_dense,
    b_raw,
    b_held,
    b_dense,
    codes,
    found_a,
    found_b,
    where_a,
    where_b,
    total,
    t_out,
    t_in,
    scale_out,
    scale_in,
    passed,
    local_sem,
    table_sem,
    b_send,
    b_recv,
    pass_send,
    pass_recv,
    term_held,
    term_scale,
    term_send,
    term_recv,
    t_send,
    t_recv,
    last_out,
    last_in,
    last_scale_out,
    last_scale_in,
    last_send,
    last_recv,
    order,
):
    pad_a, bs = a_blocks.shape[0], a_blocks.shape[1]
    pad_b = b_blocks.shape[0]
    strip = bs // STRIPS
    tile = RB * bs // TILES
    i, k = lax.axis_index("row"), lax.axis_index("col")

    def at_col(distance):
        return (i, lax.rem(k + distance + grid_cols, grid_cols))

    onward = (lax.rem(i + grid_rows - 1, grid_rows), lax.rem(k + 1, grid_cols))
    origin = (lax.rem(i + 1, grid_rows), lax.rem(k + grid_cols - 1, grid_cols))

    run, lane = grid_rows // 2, grid_cols // 2

    def passing(row, col):
        at_y = lax.rem(col, lane)
        return jnp.logical_and(lax.rem(row, run) == 0, jnp.logical_and(at_y > 0, at_y < lane - 2))

    beside = (lax.rem(i + run, grid_rows), k)
    past_beside = (lax.rem(i + run + grid_rows - 1, grid_rows), lax.rem(k + 1, grid_cols))
    passes_here = (lax.rem(i + 1 + run, grid_rows), lax.rem(k + grid_cols - 1, grid_cols))
    at_first, at_last = passing(i, k), passing(*passes_here)

    nothing = jnp.zeros((strip, bs), jnp.bfloat16)
    for held in b_held:
        for q in range(STRIPS):
            held[q][pad_b] = nothing
    a_held[pad_a] = jnp.zeros((bs, bs), jnp.bfloat16)

    barrier = pltpu.get_barrier_semaphore()
    pl.semaphore_signal(barrier, inc=1, device_id=origin, device_id_type=MESH)
    first_y, last_y = lax.rem(k, lane) < 2, lax.rem(k, lane) >= lane - 2
    for distance in (1, jnp.where(last_y, lane, 2), 3):
        pl.semaphore_signal(barrier, inc=1, device_id=at_col(distance), device_id_type=MESH)

    @pl.when(last_y)
    def _():
        pl.semaphore_signal(barrier, inc=1, device_id=at_col(2 + lane), device_id_type=MESH)

    @pl.when(at_last)
    def _():
        pl.semaphore_signal(barrier, inc=1, device_id=passes_here, device_id_type=MESH)

    @pl.when(at_first)
    def _():
        pl.semaphore_signal(barrier, inc=1, device_id=beside, device_id_type=MESH)

    loads = [
        pltpu.make_async_copy(source, target, local_sem.at[n])
        for n, (source, target) in enumerate(
            (
                (b_blocks, b_raw),
                (b_rows_hbm, b_rows),
                (b_cols_hbm, b_cols),
                (b_count_hbm, b_count),
                (a_rows_hbm, a_rows),
                (a_cols_hbm, a_cols),
                (a_count_hbm, a_count),
                (a_blocks, a_held.at[pl.ds(0, pad_a)]),
            )
        )
    ]
    for load in loads:
        load.start()

    def code_hop(s):
        return pltpu.make_async_remote_copy(
            src_ref=codes.at[s],
            dst_ref=codes.at[s + 1],
            send_sem=b_send.at[s, STRIPS],
            recv_sem=b_recv.at[s, STRIPS],
            device_id=onward,
            device_id_type=MESH,
        )

    def strip_hop(s, q):
        return pltpu.make_async_remote_copy(
            src_ref=b_held[s][q].at[pl.ds(0, pad_b)],
            dst_ref=b_held[s + 1][q].at[pl.ds(0, pad_b)],
            send_sem=b_send.at[s, q],
            recv_sem=b_recv.at[s, q],
            device_id=onward,
            device_id_type=MESH,
        )

    def hop_beside(s, n):
        return pltpu.make_async_remote_copy(
            src_ref=b_held[s][STRIPS - PER + n].at[pl.ds(0, pad_b)],
            dst_ref=passed.at[s, n],
            send_sem=b_send.at[s, STRIPS - PER + n],
            recv_sem=pass_recv.at[s, n],
            device_id=beside,
            device_id_type=MESH,
        )

    def pass_on(s, n):
        return pltpu.make_async_remote_copy(
            src_ref=passed.at[s, n],
            dst_ref=b_held[s + 1][STRIPS - PER + n].at[pl.ds(0, pad_b)],
            send_sem=pass_send.at[s, n],
            recv_sem=b_recv.at[s, STRIPS - PER + n],
            device_id=past_beside,
            device_id_type=MESH,
        )

    def start_strip(s, q):
        if q < STRIPS - PER:
            strip_hop(s, q).start()
            return

        @pl.when(at_first)
        def _():
            hop_beside(s, q - STRIPS + PER).start()

        @pl.when(jnp.logical_not(at_first))
        def _():
            strip_hop(s, q).start()

    def start_pass(s, n):
        @pl.when(at_first)
        def _():
            hop_beside(s, n).wait_recv()
            pass_on(s, n).start()

    def last_home(q):
        return (
            pltpu.make_async_remote_copy(
                src_ref=last_out.at[q],
                dst_ref=last_in.at[q],
                send_sem=last_send.at[q, 0],
                recv_sem=last_recv.at[q, 0],
                device_id=at_col(1 - STEPS),
                device_id_type=MESH,
            ),
            pltpu.make_async_remote_copy(
                src_ref=last_scale_out.at[q],
                dst_ref=last_scale_in.at[q],
                send_sem=last_send.at[q, 1],
                recv_sem=last_recv.at[q, 1],
                device_id=at_col(1 - STEPS),
                device_id_type=MESH,
            ),
        )

    def tile_rows(t):
        return pl.ds(pl.multiple_of(t * tile, tile), tile)

    def tile_home(s, h, t):
        return pltpu.make_async_remote_copy(
            src_ref=t_out.at[s - 1, h, tile_rows(t)],
            dst_ref=t_in.at[s - 1, h, tile_rows(t)],
            send_sem=t_send.at[s - 1, h, t, 0],
            recv_sem=t_recv.at[s - 1, h, t, 0],
            device_id=at_col(-s),
            device_id_type=MESH,
        )

    def scale_home(s, h, t):
        return pltpu.make_async_remote_copy(
            src_ref=scale_out.at[s - 1, h, t],
            dst_ref=scale_in.at[s - 1, h, t],
            send_sem=t_send.at[s - 1, h, t, 1],
            recv_sem=t_recv.at[s - 1, h, t, 1],
            device_id=at_col(-s),
            device_id_type=MESH,
        )

    def beside_home(h, t):
        return (
            pltpu.make_async_remote_copy(
                src_ref=t_out.at[1, h, tile_rows(t)],
                dst_ref=term_held.at[h, tile_rows(t)],
                send_sem=t_send.at[1, h, t, 0],
                recv_sem=term_recv.at[h, t, 0],
                device_id=at_col(lane - 2),
                device_id_type=MESH,
            ),
            pltpu.make_async_remote_copy(
                src_ref=scale_out.at[1, h, t],
                dst_ref=term_scale.at[h, t],
                send_sem=t_send.at[1, h, t, 1],
                recv_sem=term_recv.at[h, t, 1],
                device_id=at_col(lane - 2),
                device_id_type=MESH,
            ),
        )

    def passed_home(h, t):
        return (
            pltpu.make_async_remote_copy(
                src_ref=term_held.at[h, tile_rows(t)],
                dst_ref=t_in.at[1, h, tile_rows(t)],
                send_sem=term_send.at[h, t, 0],
                recv_sem=t_recv.at[1, h, t, 0],
                device_id=at_col(lane),
                device_id_type=MESH,
            ),
            pltpu.make_async_remote_copy(
                src_ref=term_scale.at[h, t],
                dst_ref=scale_in.at[1, h, t],
                send_sem=term_send.at[h, t, 1],
                recv_sem=t_recv.at[1, h, t, 1],
                device_id=at_col(lane),
                device_id_type=MESH,
            ),
        )

    def start_home(s, h, t):
        def straight():
            scale_home(s, h, t).start()
            tile_home(s, h, t).start()

        if s != 2:
            straight()
            return

        @pl.when(first_y)
        def _():
            for copy in beside_home(h, t):
                copy.start()

        pl.when(jnp.logical_not(first_y))(straight)

    def pass_home(h):
        @pl.when(last_y)
        def _():
            for t in range(TILES):
                for copy in beside_home(h, t):
                    copy.wait_recv()
                for copy in passed_home(h, t):
                    copy.start()

    loads[0].wait()

    def turn(q):
        def turn_block(p, carry):
            b_held[0][q][p] = b_raw[p, :, q * strip : (q + 1) * strip].T
            return carry

        lax.fori_loop(0, pad_b, turn_block, 0, unroll=True)

    turn(0)
    for load in loads[1:4]:
        load.wait()
    codes[0] = jnp.full((8, 128), -1, jnp.int32)
    codes[0, 0:1, 0:pad_b] = slot_codes(b_rows, b_cols, b_count, CB)

    pl.semaphore_wait(barrier, STEPS + jnp.where(at_first, 2, 0) + jnp.where(last_y, 1, 0))
    code_hop(0).start()
    start_strip(0, 0)
    for q in range(1, STRIPS):
        turn(q)
        start_strip(0, q)

    stands = lax.broadcasted_iota(jnp.int32, order.shape, 0)
    belongs = lax.broadcasted_iota(jnp.int32, order.shape, 1)
    strip_of, rest = stands // (CB * strip), stands % (CB * strip)
    goes = rest // strip * bs + strip_of * strip + rest % strip
    order[...] = jnp.where(belongs == goes, 1.0, 0.0).astype(jnp.bfloat16)

    for load in loads[4:7]:
        load.wait()
    found_a[...] = slot_of_block(slot_codes(a_rows, a_cols, a_count, KB), RB * KB, pad_a)
    a_table = pltpu.make_async_copy(found_a, where_a, table_sem.at[STEPS])
    a_table.start()

    def b_table(s):
        return pltpu.make_async_copy(found_b.at[s], where_b.at[s], table_sem.at[s])

    def find_b(s):
        found_b[s] = slot_of_block(codes[s, 0:1, :], KB * CB, pad_b)
        b_table(s).start()

    find_b(0)
    a_table.wait()
    loads[7].wait()

    def place_a(p, carry):
        r, c = p // KB, p % KB
        a_dense[
            pl.ds(pl.multiple_of(r * bs, bs), bs), pl.ds(pl.multiple_of(c * bs, bs), bs)
        ] = a_held[where_a[p, 0]]
        return carry

    lax.fori_loop(0, RB * KB, place_a, 0, unroll=8)

    def place_b(s, strips):
        def place(r, carry):
            for c in range(CB):
                slot = where_b[s, r * CB + c, 0]
                for q in strips:
                    first = (q % PER * CB + c) * strip
                    b_dense[
                        q // PER, first : first + strip, pl.ds(pl.multiple_of(r * bs, bs), bs)
                    ] = b_held[s][q][slot]
            return carry

        lax.fori_loop(0, KB, place, 0, unroll=4)

    def product(h, t):
        return lax.dot_general(
            a_dense[tile_rows(t), :],
            b_dense[h],
            (((1,), (1,)), ((), ())),
            preferred_element_type=jnp.float32,
        )

    def coded(term):
        largest = jnp.maximum(jnp.max(jnp.abs(term), axis=0, keepdims=True), 1e-30)
        code = jnp.round(term * (32767.0 / largest)).astype(jnp.int32).astype(jnp.int16)
        return code, largest * (1.0 / 32767.0)

    def send_last(q):
        first = q % PER * CB * strip
        parts = [
            lax.dot_general(
                a_dense[t * tile : (t + 1) * tile, :],
                b_dense[q // PER, first : first + CB * strip, :],
                (((1,), (1,)), ((), ())),
                preferred_element_type=jnp.float32,
            )
            for t in range(TILES)
        ]
        last_out[q], last_scale_out[q] = coded(jnp.concatenate(parts, axis=1))
        for copy in last_home(q):
            copy.start()

    def last_terms(h):
        terms = []
        for q in range(h * PER, (h + 1) * PER):
            for copy in last_home(q):
                copy.wait_recv()
            terms.append(last_in[q].astype(jnp.float32) * last_scale_in[q])
        wide = CB * strip
        return [
            jnp.concatenate([term[:, t * wide : (t + 1) * wide] for term in terms], axis=1)
            for t in range(TILES)
        ]

    def own_tile(h, t, carry):
        total[h, tile_rows(t), :] = product(h, t)
        return carry

    def sent_tile(s, h, t, carry):
        term = product(h, t)
        t_out[s - 1, h, tile_rows(t), :], scale_out[s - 1, h, t] = coded(term)
        start_home(s, h, t)
        return carry

    def term_from(s, h, t):
        scale_home(s, h, t).wait_recv()
        tile_home(s, h, t).wait_recv()
        return t_in[s - 1, h, tile_rows(t), :].astype(jnp.float32) * scale_in[s - 1, h, t]

    def add_tile(s, h, t, carry):
        total[h, tile_rows(t), :] = total[h, tile_rows(t), :] + term_from(s, h, t)
        return carry

    def strips_of(h):
        return range(h * PER, (h + 1) * PER)

    b_table(0).wait()
    for h in range(HALVES):
        place_b(0, strips_of(h))
        lax.fori_loop(0, TILES, functools.partial(own_tile, h), 0)

    for s in range(1, STEPS):
        code_hop(s - 1).wait_recv()
        if s < STEPS - 1:
            code_hop(s).start()
        find_b(s)
        b_table(s).wait()
        for q in range(STRIPS):
            if q < PER:
                start_pass(s - 1, q)
            strip_hop(s - 1, q).wait_recv()
            if s == STEPS - 1:
                place_b(s, [q])
                send_last(q)
            else:
                start_strip(s, q)
            h = q // PER
            if q % PER < PER - 1:
                continue
            if s == STEPS - 1:
                pass_home(h)
            else:
                place_b(s, strips_of(h))
                lax.fori_loop(0, TILES, functools.partial(sent_tile, s, h), 0)

    for s in range(1, STEPS - 1):
        for h in range(HALVES):
            lax.fori_loop(0, TILES, functools.partial(add_tile, s, h), 0)

    for h in range(HALVES - 1):
        for t, term in enumerate(last_terms(h)):
            total[h, t * tile : (t + 1) * tile, :] = total[h, t * tile : (t + 1) * tile, :] + term

    for t, term in enumerate(last_terms(HALVES - 1)):
        rows = slice(t * tile, (t + 1) * tile)
        whole = [total[h, rows, :] for h in range(HALVES - 1)] + [total[HALVES - 1, rows, :] + term]
        whole = jnp.concatenate([half.astype(jnp.bfloat16) for half in whole], axis=1)
        out_ref[rows, :] = jnp.dot(whole, order[...], preferred_element_type=jnp.float32).astype(jnp.bfloat16)

    @pl.when(at_first)
    def _():
        for s in range(STEPS - 1):
            for n in range(PER):
                pass_on(s, n).wait_send()

    @pl.when(last_y)
    def _():
        for h in range(HALVES):
            for t in range(TILES):
                for copy in passed_home(h, t):
                    copy.wait_send()

    for s in range(STEPS - 1):
        code_hop(s).wait_send()
        for q in range(STRIPS):
            strip_hop(s, q).wait_send()
    for s in range(1, STEPS - 1):
        for h in range(HALVES):
            for t in range(TILES):
                tile_home(s, h, t).wait_send()
                scale_home(s, h, t).wait_send()
    for q in range(STRIPS):
        for copy in last_home(q):
            copy.wait_send()


def per_device(a_blocks, a_rows, a_cols, a_count, b_blocks, b_rows, b_cols, b_count):
    grid_rows, grid_cols = lax.axis_size("row"), lax.axis_size("col")
    pad_a, bs = a_blocks.shape[2], a_blocks.shape[3]
    pad_b = b_blocks.shape[2]
    vmem = pl.BlockSpec(memory_space=pltpu.VMEM)
    whole = pl.BlockSpec(memory_space=pltpu.HBM)
    rows, depth, columns = RB * bs, KB * bs, CB * bs
    strip, wide = bs // STRIPS, columns // HALVES
    return pl.pallas_call(
        functools.partial(kernel, grid_rows, grid_cols),
        out_shape=pltpu.VMEM((rows, columns), jnp.bfloat16),
        in_specs=[whole] * 8,
        out_specs=vmem,
        scratch_shapes=[
            pltpu.VMEM((1, pad_a), jnp.int32),
            pltpu.VMEM((1, pad_a), jnp.int32),
            pltpu.VMEM((1, 1), jnp.int32),
            pltpu.VMEM((1, pad_b), jnp.int32),
            pltpu.VMEM((1, pad_b), jnp.int32),
            pltpu.VMEM((1, 1), jnp.int32),
            pltpu.VMEM((pad_a + 1, bs, bs), jnp.bfloat16),
            pltpu.VMEM((rows, depth), jnp.bfloat16),
            pltpu.VMEM((pad_b, bs, bs), jnp.bfloat16),
            [[pltpu.VMEM((pad_b + 1, strip, bs), jnp.bfloat16)] * STRIPS] * STEPS,
            pltpu.VMEM((HALVES, wide, depth), jnp.bfloat16),
            pltpu.VMEM((STEPS, 8, 128), jnp.int32),
            pltpu.VMEM((RB * KB, 128), jnp.int32),
            pltpu.VMEM((STEPS, KB * CB, 128), jnp.int32),
            pltpu.SMEM((RB * KB, 128), jnp.int32),
            pltpu.SMEM((STEPS, KB * CB, 128), jnp.int32),
            pltpu.VMEM((HALVES, rows, wide), jnp.float32),
            pltpu.VMEM((STEPS - 2, HALVES, rows, wide), jnp.int16),
            pltpu.VMEM((STEPS - 2, HALVES, rows, wide), jnp.int16),
            pltpu.VMEM((STEPS - 2, HALVES, TILES, 1, wide), jnp.float32),
            pltpu.VMEM((STEPS - 2, HALVES, TILES, 1, wide), jnp.float32),
            pltpu.VMEM((STEPS - 1, PER, pad_b, strip, bs), jnp.bfloat16),
            pltpu.SemaphoreType.DMA((8,)),
            pltpu.SemaphoreType.DMA((STEPS + 1,)),
            pltpu.SemaphoreType.DMA((STEPS - 1, STRIPS + 1)),
            pltpu.SemaphoreType.DMA((STEPS - 1, STRIPS + 1)),
            pltpu.SemaphoreType.DMA((STEPS - 1, PER)),
            pltpu.SemaphoreType.DMA((STEPS - 1, PER)),
            pltpu.VMEM((HALVES, rows, wide), jnp.int16),
            pltpu.VMEM((HALVES, TILES, 1, wide), jnp.float32),
            pltpu.SemaphoreType.DMA((HALVES, TILES, 2)),
            pltpu.SemaphoreType.DMA((HALVES, TILES, 2)),
            pltpu.SemaphoreType.DMA((STEPS - 2, HALVES, TILES, 2)),
            pltpu.SemaphoreType.DMA((STEPS - 2, HALVES, TILES, 2)),
            pltpu.VMEM((STRIPS, rows // TILES, TILES * CB * strip), jnp.int16),
            pltpu.VMEM((STRIPS, rows // TILES, TILES * CB * strip), jnp.int16),
            pltpu.VMEM((STRIPS, 1, TILES * CB * strip), jnp.float32),
            pltpu.VMEM((STRIPS, 1, TILES * CB * strip), jnp.float32),
            pltpu.SemaphoreType.DMA((STRIPS, 2)),
            pltpu.SemaphoreType.DMA((STRIPS, 2)),
            pltpu.VMEM((columns, columns), jnp.bfloat16),
        ],
        compiler_params=pltpu.CompilerParams(
            collective_id=0, has_side_effects=True, vmem_limit_bytes=60 * 1024 * 1024
        ),
    )(
        a_rows.reshape(1, pad_a),
        a_cols.reshape(1, pad_a),
        a_count,
        b_rows.reshape(1, pad_b),
        b_cols.reshape(1, pad_b),
        b_count,
        a_blocks.reshape(pad_a, bs, bs),
        b_blocks.reshape(pad_b, bs, bs),
    )


def solution(mesh):
    placed = (
        P("row", "col", None, None, None),
        P("row", "col", None),
        P("row", "col", None),
        P("row", "col"),
        P("row", "col", None, None, None),
        P("row", "col", None),
        P("row", "col", None),
        P("row", "col"),
    )
    return jax.shard_map(
        per_device, mesh=mesh, in_specs=placed, out_specs=P("row", "col"), check_vma=False
    )
```
